256 devices in a mesh: slab: 32 (over z, y), coil: 8 (over x, core).
Axes of the slice: x: 4, y: 4, z: 8, core: 2. Of those that a mesh axis runs over, the one named last changes fastest.
Arguments:
- noisy_image: float32 [2, 32, 320, 320], P(None, 'slab', 'coil'), may hold values from -6 to 6
- noise_draw: float32 [2, 32, 320, 320], P(None, 'slab', 'coil'), may hold values from -6 to 6
- block_routes: int32 [32, 40], P('slab'), may hold values from -1 to 7, as said below
- conv_in: bfloat16 [9, 128, 2], replicated, may hold values from -1.5 to 1.5
- bias_in: float32 [128], replicated, may hold values from -6 to 6
- norm_gain: float32 [128], replicated, may hold values from 0.3 to 1.7
- conv_mid: bfloat16 [9, 128, 128], replicated, may hold values from -0.1875 to 0.1875
- bias_mid: float32 [128], replicated, may hold values from -6 to 6
- conv_out: bfloat16 [9, 2, 128], replicated, may hold values from -0.1875 to 0.1875
- coil_maps: float32 [2, 16, 32, 320, 320], P(None, 'coil', None, 'slab'), may hold values from -1 to 1
- kspace_data: float32 [2, 16, 32, 320, 320], P(None, 'coil', None, 'slab'), may hold values from -6 to 6
- sample_mask: int32 [320, 320], P('slab'), may hold values 0 or 1
Outputs:
- prior_step: float32 [2, 32, 320, 320], P(None, 'slab', 'coil')
- refined: float32 [2, 32, 320, 320], P(None, 'coil', None, 'slab')
The draws below stay inside these ranges and needn't reach their ends.
Inputs may be any that keep to these rules, and one draw needn't show every extreme that they name: block_routes[z, b] is -1 where row block b of slice z is background and otherwise the index along coil of the device that computes it; the foreground blocks of a slice are consecutive; of the 5 blocks of a slice held by one index of coil at most 1 go to any one index, and each index computes at most 3 blocks of a slice; both bounds are reached in some slice.
All inputs are finite; a program needn't handle non-finite values. No bound on the sum of `sample_mask` on one device may be relied on, other than what follows from the above.
Results may differ from the reference program's by a relative error of at most 0.0017.
Values may be sent and summed in bfloat16 or wider, within the bound.
A program may use at most 128 MiB of HBM per device.

```python
import math
import jax
import jax.numpy as jnp
from jax import lax

H = 320
W = 320
NF = 128
COILS = 16
RB = 8
ITERS = 2
Z = 32
NBLK = 40
LOAD = 3
N_COIL = 8


def draw_block_routes(key, part):
    key = jax.random.fold_in(key, 11)
    capacity = min(N_COIL * LOAD, NBLK)
    keys = jax.random.split(key, 4)
    counted = jax.random.randint(keys[0], (Z,), max(1, capacity // 4), capacity + 1)
    counted = counted.at[Z // 2].set(capacity)
    starting = jax.random.randint(keys[1], (Z,), 0, NBLK - counted + 1)
    offsets = jax.random.randint(keys[2], (Z,), 0, N_COIL)
    orders = jax.vmap(lambda one_key: jax.random.permutation(one_key, N_COIL))(jax.random.split(keys[3], Z))
    block_index = jnp.arange(NBLK, dtype=jnp.int32)[None, :]
    relative = block_index - starting[:, None]
    inside_fg = (relative >= 0) & (relative < counted[:, None])
    position = (relative + offsets[:, None]) % N_COIL
    targets = jnp.take_along_axis(orders, position, axis=1)
    return jnp.where(inside_fg, targets, -1).astype(jnp.int32)


def plant(values, rng, low, largest):
    longest = values.shape.index(max(values.shape))
    spots = []
    for shift in (0, 1):
        where = [jax.random.randint(jax.random.fold_in(rng, axis), (), 0, length) for axis, length in enumerate(values.shape)]
        where[longest] = (where[longest] + shift) % values.shape[longest]
        spots.append(tuple(where))
    return values.at[spots[0]].set(low).at[spots[1]].set(largest)


def steps_of(own_key, shape, cuts, low, top_value):
    loudness, own = 1.0, jax.random.fold_in(own_key, 6)
    for axis_at, shards_of in cuts:
        draws = jnp.exp(jax.random.uniform(jax.random.fold_in(own, axis_at), (shards_of,), jnp.float32, low / len(cuts), top_value / len(cuts)))
        loudness = loudness * jnp.repeat(draws, shape[axis_at] // shards_of).reshape([-1 if axis == axis_at else 1 for axis in range(len(shape))])
    return loudness


def noise(rng, extent, spread, limit, cuts=(), kind=jnp.bfloat16):
    entries = jax.random.normal(rng, extent, jnp.float32) * spread
    if len(cuts) > 0:
        entries = steps_of(rng, extent, cuts, -0.22, 0.18) * entries
    return jnp.clip(entries, min=-limit, max=limit).astype(kind)


def setup_inputs(seed: int = 0) -> dict:
    key_of = jax.random.split(jax.random.key(seed), 13)
    return {
        "noisy_image": noise(key_of[0], (2, Z, H, W), 1.0, 6.0, ((1, 32), (2, 8)), jnp.float32),
        "noise_draw": noise(key_of[1], (2, Z, H, W), 1.0, 6.0, ((1, 32), (2, 8)), jnp.float32),
        "block_routes": draw_block_routes(jax.random.fold_in(key_of[12], 71), 0),
        "conv_in": noise(key_of[3], (9, NF, 2), 18 ** -0.5, 1.5),
        "bias_in": noise(key_of[4], (NF,), 1.0, 6.0, (), jnp.float32),
        "norm_gain": jnp.clip(jax.random.uniform(key_of[5], (NF,), jnp.float32, 0.3, 1.7), 0.3, 1.7),
        "conv_mid": noise(key_of[6], (9, NF, NF), (9 * NF) ** -0.5, 0.1875),
        "bias_mid": noise(key_of[7], (NF,), 1.0, 6.0, (), jnp.float32),
        "conv_out": noise(key_of[8], (9, 2, NF), (9 * NF) ** -0.5, 0.1875),
        "coil_maps": noise(key_of[9], (2, COILS, Z, W, H), 0.18, 1.0, ((1, 8), (3, 32)), jnp.float32),
        "kspace_data": noise(key_of[10], (2, COILS, Z, H, W), 1.0, 6.0, ((1, 8), (3, 32)), jnp.float32),
        "sample_mask": plant((jax.random.randint(key_of[11], (H, W), 0, 4) < 1).astype(jnp.int32), jax.random.fold_in(key_of[11], 1), 0, 1),
    }


SIGMA_NOW = 1.0
SIGMA_NEXT = 0.8
STEP_VARIANCE = SIGMA_NOW * SIGMA_NOW - SIGMA_NEXT * SIGMA_NEXT
STEP_SCALE = math.sqrt(STEP_VARIANCE)
STEP_SIZE = 0.4
PENALTY = 0.5
SHRINK = 0.3
EPSILON = 1e-05

def conv_same(feature, weight):
    height, columns = (feature.shape[1], feature.shape[2])
    padded = jnp.pad(feature.astype(jnp.float32), ((0, 0), (1, 1), (1, 1)))
    running = jnp.zeros((weight.shape[1], height, columns), jnp.float32)
    for tap_index in range(9):
        row_tap, column_tap = (tap_index // 3, tap_index % 3)
        window = padded[:, row_tap:row_tap + height, column_tap:column_tap + columns]
        running = running + jnp.einsum('oc,chw->ohw', weight[tap_index].astype(jnp.float32), window)
    return running

def local_difference(volume):
    return jnp.concatenate([volume[:, 1:] - volume[:, :-1], jnp.zeros_like(volume[:, :1])], axis=1)

def local_transpose(values):
    return jnp.concatenate([-values[:, :1], values[:, :-2] - values[:, 1:-1], values[:, -2:-1]], axis=1)

def reference(noisy_image, noise_draw, block_routes, conv_in, bias_in, norm_gain, conv_mid, bias_mid, conv_out, coil_maps, kspace_data, sample_mask):
    keep_rows = jnp.repeat((block_routes >= 0).astype(jnp.float32), RB, axis=1)

    def one_slice(inputs):
        slice_pair, keep_slice = inputs
        net_input = slice_pair.astype(jnp.bfloat16)
        first_layer = conv_same(net_input, conv_in) + bias_in[:, None, None]
        first_state = lax.optimization_barrier(first_layer.astype(jnp.bfloat16)).astype(jnp.float32)
        inverse_rms = lax.rsqrt(lax.optimization_barrier(jnp.mean(first_state * first_state, axis=0, keepdims=True)) + EPSILON)
        active = jax.nn.silu(first_state * inverse_rms * norm_gain[:, None, None]).astype(jnp.bfloat16)
        second = conv_same(active, conv_mid) + first_state + bias_mid[:, None, None]
        second_state = lax.optimization_barrier(second.astype(jnp.bfloat16)).astype(jnp.float32)
        second_active = jax.nn.silu(second_state).astype(jnp.bfloat16)
        output = (conv_same(second_active, conv_out) / SIGMA_NOW).astype(jnp.bfloat16)
        return output * keep_slice[None, :, None].astype(jnp.bfloat16)
    scores = lax.map(one_slice, (jnp.moveaxis(noisy_image, 1, 0), keep_rows))
    prior_step = noisy_image + STEP_VARIANCE * jnp.moveaxis(scores, 0, 1).astype(jnp.float32) + STEP_SCALE * noise_draw
    maps_complex = jnp.swapaxes(lax.complex(coil_maps[0], coil_maps[1]), -1, -2)
    data_complex = lax.complex(kspace_data[0], kspace_data[1])
    weights = sample_mask.astype(jnp.float32)

    def adjoint_step(carry, inputs):
        coil_map, measured = inputs
        returned = jnp.fft.ifft2(weights * measured, norm='ortho')
        return (carry + jnp.conj(coil_map) * returned, None)
    adjoint, _ = lax.scan(adjoint_step, jnp.zeros_like(maps_complex[0]), (maps_complex, data_complex))

    def data_term(volume):
        current = lax.complex(volume[0], volume[1])

        def normal_step(carry, coil_map):
            spectrum = weights * jnp.fft.fft2(coil_map * current, norm='ortho')
            return (carry + jnp.conj(coil_map) * jnp.fft.ifft2(spectrum, norm='ortho'), None)
        summed, _ = lax.scan(normal_step, jnp.zeros_like(current), maps_complex)
        residual = summed - adjoint
        return jnp.stack([jnp.real(residual), jnp.imag(residual)])
    volume = prior_step
    ahead_diff = local_difference(volume)
    slack_part = jnp.zeros_like(volume)
    dual_part = jnp.zeros_like(volume)
    for step_index in range(ITERS):
        gradient = data_term(volume) + PENALTY * local_transpose(ahead_diff - slack_part + dual_part)
        volume = volume - STEP_SIZE * gradient
        if step_index + 1 < ITERS:
            ahead_diff = local_difference(volume)
            shifted = ahead_diff + dual_part
            slack_part = shifted - jnp.clip(shifted, -SHRINK, SHRINK)
            dual_part = shifted - slack_part
    return (prior_step, volume)
```

```python
import functools
import math

import jax
import jax.numpy as jnp
import numpy as np
from jax import lax
from jax.experimental import pallas as pl
from jax.experimental.pallas import tpu as pltpu
from jax.sharding import PartitionSpec as P

NS, NC, NZ, NY = 32, 8, 8, 4
N = 320
LP = 384
R = 40
STEP_VARIANCE = 1.0 - 0.8 * 0.8
STEP_SCALE = math.sqrt(STEP_VARIANCE)
STEP_SIZE = 0.4
PENALTY = 0.5
SHRINK = 0.3
EPSILON = 1e-05
F32, BF16 = jnp.float32, jnp.bfloat16
MESH = pl.DeviceIdType.MESH
OFFSETS = [(dz, dy) for dz in range(NZ) for dy in range(NY) if (dz, dy) != (0, 0)]


def dft_tables():
    index = np.arange(N)
    angle = (index[:, None] * index[None, :] % N) * (2.0 * math.pi / N)
    cosine, sine = np.cos(angle) / math.sqrt(N), np.sin(angle) / math.sqrt(N)

    def left(sign):
        return np.block([[cosine, sign * sine], [-sign * sine, cosine]])

    def right(sign):
        table = np.zeros((2 * LP, 2 * LP))
        table[:N, :N] = table[LP : LP + N, LP : LP + N] = cosine
        table[:N, LP : LP + N] = -sign * sine
        table[LP : LP + N, :N] = sign * sine
        return table

    def split(table):
        import ml_dtypes

        high = table.astype(ml_dtypes.bfloat16)
        return high, (table - high.astype(np.float64)).astype(ml_dtypes.bfloat16)

    left_fwd, left_inv = split(left(1.0))[0], split(left(-1.0))
    right_fwd, right_inv = split(right(1.0))[0], split(right(-1.0))
    return left_fwd, left_inv[0], left_inv[1], right_fwd, right_inv[0], right_inv[1]


def silu(value):
    return value * (0.5 + 0.5 * jnp.tanh(0.5 * value))


def mm(a, b):
    return jnp.dot(a, b, preferred_element_type=F32)


def split_f32(value):
    high = value.astype(BF16)
    return high, (value - high.astype(F32)).astype(BF16)


def kernel(
    noisy, noise, routes, w_in, b_in, gain, w_mid, b_mid, w_out, mask_in,
    maps_hbm, kdata_hbm, lf_hbm, li_hbm, lil_hbm, rf_hbm, ri_hbm, ril_hbm,
    prior, out,
    maps, kdata, lf, li, lil, rf, rinv, ril,
    msg, got, halo_out, halo_in, x_nat, x_t, x3, act3, first, acc,
    ag0_out, ag0_in, v, zex0_in, zex1_out, zex1_in,
    kn, mask_n, kt, mask_t, gadj, sens, adj,
    stage_a, stage_b, rs_out, rs_in, ag_out, ag_in, fin_out,
    load_sem, halo_ss, halo_rs, a_ss, a_rs, ag0_ss, ag0_rs, z_ss, z_rs,
    rs_ss, rs_rs, ag_ss, ag_rs, fin_ss, fin_rs, local_sem,
):
    s, c = lax.axis_index("slab"), lax.axis_index("coil")
    z, y = s // NY, lax.rem(s, NY)
    loads = [
        pltpu.make_async_copy(src, dst, load_sem.at[i])
        for i, (src, dst) in enumerate(
            [(kdata_hbm, kdata), (maps_hbm, maps), (lf_hbm, lf), (li_hbm, li), (lil_hbm, lil),
             (rf_hbm, rf), (ri_hbm, rinv), (ril_hbm, ril)]
        )
    ]
    for load in loads:
        load.start()

    barrier = pltpu.get_barrier_semaphore()
    coil_peers = [lax.rem(c + k, NC) for k in range(1, NC)]
    slab_to = [lax.rem(z + dz, NZ) * NY + lax.rem(y + dy, NY) for dz, dy in OFFSETS]
    for peer in coil_peers:
        pl.semaphore_signal(barrier, inc=1, device_id=(s, peer), device_id_type=MESH)
    for peer in slab_to:
        pl.semaphore_signal(barrier, inc=1, device_id=(peer, c), device_id_type=MESH)

    x_nat[...] = jnp.zeros_like(x_nat)
    for ch in range(2):
        rows = noisy[ch, 0].astype(BF16).astype(F32)
        x_nat[ch * 64 + 3 : ch * 64 + 43, 0:N] = rows
        halo_out[0, ch * 8 : ch * 8 + 3, :] = rows[0:3]
        halo_out[1, ch * 8 : ch * 8 + 3, :] = rows[R - 3 : R]

    def beside(real, imag):
        return jnp.concatenate(
            [real[:, 0:256], imag[:, 0:256], jnp.concatenate([real[:, 256:N], imag[:, 256:N]], axis=1)], axis=1
        )

    mask_f = mask_in[...].astype(F32)
    mask_rows = jnp.concatenate([beside(mask_f[0:5], mask_f[5:10]), jnp.zeros((3, 2 * N), F32)], axis=0)
    loads[0].wait()
    loads[1].wait()

    def pack(dest, carry):
        pieces = [beside(maps[0, j, dest], maps[1, j, dest]) for j in range(2)]
        pieces += [beside(kdata[0, j, dest], kdata[1, j, dest]) for j in range(2)]
        msg[dest] = jnp.concatenate(pieces + [mask_rows], axis=0).astype(BF16)
        return carry

    lax.fori_loop(0, NS, pack, 0)

    pl.semaphore_wait(barrier, NC - 1 + NS - 1)

    up, down = lax.rem(c + NC - 1, NC), lax.rem(c + 1, NC)
    halo = []
    for side, peer in ((0, up), (1, down)):
        copy = pltpu.make_async_remote_copy(
            src_ref=halo_out.at[side], dst_ref=halo_in.at[side], send_sem=halo_ss.at[side],
            recv_sem=halo_rs.at[side], device_id=(s, peer), device_id_type=MESH)
        copy.start()
        halo.append(copy)

    sent = [[], []]
    for part, (low, count) in enumerate(((16, 32), (0, 16))):
        for i, peer in enumerate(slab_to):
            copy = pltpu.make_async_remote_copy(
                src_ref=msg.at[peer, pl.ds(low, count)], dst_ref=got.at[s, pl.ds(low, count)],
                send_sem=a_ss.at[part, i], recv_sem=a_rs.at[part, i], device_id=(peer, c), device_id_type=MESH)
            copy.start()
            sent[part].append(copy)
    own_copy = pltpu.make_async_copy(msg.at[s], got.at[s], local_sem.at[0])
    own_copy.start()

    for copy in halo:
        copy.wait()
    for ch in range(2):
        above = jnp.where(c > 0, halo_in[1, ch * 8 : ch * 8 + 3, :], 0.0)
        below = jnp.where(c < NC - 1, halo_in[0, ch * 8 : ch * 8 + 3, :], 0.0)
        x_nat[ch * 64 : ch * 64 + 3, 0:N] = above
        x_nat[ch * 64 + 43 : ch * 64 + 46, 0:N] = below
    x_t[0:8, :] = jnp.zeros((8, 128), F32)
    x_t[8 : 8 + LP, :] = x_nat[...].T
    for b in range(3):
        x3[:, b * 128 : b * 128 + 128] = x_t[7 + b : 7 + b + N, :].astype(BF16)

    column = lax.broadcasted_iota(jnp.int32, (N, 128), 0)

    def shifted(value, offset):
        if offset == 0:
            return value
        if offset < 0:
            return jnp.where(column == 0, 0.0, pltpu.roll(value, 1, 0))
        return jnp.where(column == N - 1, 0.0, pltpu.roll(value, N - 1, 0))

    def inside(row):
        return jnp.where(jnp.logical_and(row >= 0, row < N), 1.0, 0.0).astype(F32)

    def first_pair(pair, carry):
        q = 2 * pair
        weights = jnp.concatenate(
            [pltpu.roll(w_in[...], q, 0), pltpu.roll(w_in[...], q + 1, 0)], axis=1).astype(BF16)
        both = mm(x3[...], weights)
        for half in range(2):
            state = (both[:, half * 128 : half * 128 + 128] + b_in[...]).astype(BF16)
            first[q + half] = state
            state = state.astype(F32)
            scale = lax.rsqrt(jnp.mean(state * state, axis=-1, keepdims=True) + EPSILON)
            active = silu(state * scale * gain[...]) * inside(c * R - 2 + q + half)
            for b in range(3):
                at = pl.multiple_of((q + half) * LP + b * 128, 128)
                act3[:, pl.ds(at, 128)] = shifted(active, b - 1).astype(BF16)
        return carry

    lax.fori_loop(0, 22, first_pair, 0)

    acc[...] = jnp.zeros_like(acc)

    def second_pair(pair, carry):
        p = 2 * pair
        both = mm(act3[:, pl.ds(pl.multiple_of(p * LP, 128), 4 * LP)], w_mid[...])
        halves, weights = [], []
        for half in range(2):
            second = first[p + half + 1].astype(F32) + both[:, half * 128 : half * 128 + 128] + b_mid[...]
            second = second.astype(BF16).astype(F32)
            halves.append((silu(second) * inside(c * R - 1 + p + half)).astype(BF16))
            weights.append(jnp.concatenate(
                [pltpu.roll(w_out[:, b * 128 : b * 128 + 128], lax.rem(p + half + 126, 128), 1) for b in range(3)],
                axis=1))
        acc[...] += mm(jnp.concatenate(halves, axis=1), jnp.concatenate(weights, axis=0).astype(BF16))
        return carry

    lax.fori_loop(0, 21, second_pair, 0)

    score_t = shifted(acc[:, 0:128], -1) + acc[:, 128:256] + shifted(acc[:, 256:384], 1)
    x_t[0:N, :] = score_t
    score = x_t[0:LP, :].T
    block = lax.broadcasted_iota(jnp.int32, (R, 40), 1)
    block_of_row = c * 5 + lax.broadcasted_iota(jnp.int32, (R, 40), 0) // 8
    routed = jnp.where(routes[...] >= 0, 1.0, 0.0).astype(F32)
    keep = jnp.sum(jnp.where(block == block_of_row, jnp.broadcast_to(routed, (R, 40)), 0.0), axis=1, keepdims=True)
    for ch in range(2):
        value = score[ch * 64 : ch * 64 + R, 0:N].astype(BF16).astype(F32) * keep
        stepped = noisy[ch, 0] + STEP_VARIANCE * value + STEP_SCALE * noise[ch, 0]
        prior[ch, 0] = stepped
        ag0_out[ch * R : ch * R + R, :] = stepped

    def to_coil(src_of, dst, send_sems, recv_sems):
        copies = []
        for i, peer in enumerate(coil_peers):
            copy = pltpu.make_async_remote_copy(
                src_ref=src_of(peer), dst_ref=dst.at[c], send_sem=send_sems.at[i],
                recv_sem=recv_sems.at[i], device_id=(s, peer), device_id_type=MESH)
            copy.start()
            copies.append(copy)
        return copies

    gathered = to_coil(lambda peer: ag0_out, ag0_in, ag0_ss, ag0_rs)
    ag0_in[c] = ag0_out[...]
    x_nat[...] = jnp.zeros_like(x_nat)
    for copy in gathered:
        copy.wait()
    kn[...] = jnp.zeros_like(kn)
    for ch in range(2):
        for peer in range(NC):
            kn[ch, peer * R : peer * R + R, 0:N] = ag0_in[peer, ch * R : ch * R + R, :]
        v[ch] = kn[ch].T[0:N, :]

    def own_chunk():
        at = pl.multiple_of(c * R, 8)
        return [v[ch, pl.ds(at, R), :] for ch in range(2)]

    def to_neighbours(number, src, dst):
        copies = []
        for side, peer in ((0, lax.rem(s + NS - 1, NS)), (1, lax.rem(s + 1, NS))):
            copy = pltpu.make_async_remote_copy(
                src_ref=src, dst_ref=dst.at[side], send_sem=z_ss.at[number, side],
                recv_sem=z_rs.at[number, side], device_id=(peer, c), device_id_type=MESH)
            copy.start()
            copies.append(copy)
        return copies

    state = own_chunk()
    for ch in range(2):
        zex1_out[0, ch * R : ch * R + R, :] = state[ch]
    neighbours = to_neighbours(0, zex1_out.at[0], zex0_in)

    def regular(state, received, clip):
        result = []
        for ch in range(2):
            behind = received[1, ch * R : ch * R + R, :]
            ahead = received[0, ch * R : ch * R + R, :]
            low, high = state[ch] - behind, ahead - state[ch]
            if clip:
                low, high = 2.0 * jnp.clip(low, -SHRINK, SHRINK), 2.0 * jnp.clip(high, -SHRINK, SHRINK)
            result.append(jnp.where(s > 0, low, 0.0) - jnp.where(s < NS - 1, high, 0.0))
        return result

    lane = lax.broadcasted_iota(jnp.int32, (R, 128), 1)

    def apart(rows):
        tail = rows[:, 512:640]
        zero = jnp.zeros_like(tail)
        real_tail = jnp.where(lane[: rows.shape[0]] < 64, tail, zero)
        imag_tail = jnp.where(lane[: rows.shape[0]] < 64, pltpu.roll(tail, 64, 1), zero)
        return (jnp.concatenate([rows[:, 0:256], real_tail], axis=1),
                jnp.concatenate([rows[:, 256:512], imag_tail], axis=1))

    own_copy.wait()
    for copy in sent[0]:
        copy.wait_recv()
    mask_n[...] = jnp.zeros_like(mask_n)
    kn[...] = jnp.zeros_like(kn)

    def unpack_k(group, carry):
        rows = [got[group * NY + i, 16:48, :].astype(F32) for i in range(NY)]
        at = pl.multiple_of(group * R, 8)
        marks = [apart(part[24:29]) for part in rows]
        marks = jnp.concatenate([half for pair in marks for half in pair], axis=0)
        mask_n[pl.ds(at, R), :] = marks
        for j in range(2):
            real, imag = apart(jnp.concatenate([part[4 + 10 * j : 14 + 10 * j] for part in rows], axis=0))
            kn[2 * j, pl.ds(at, R), :] = real * marks
            kn[2 * j + 1, pl.ds(at, R), :] = imag * marks
        return carry

    lax.fori_loop(0, NZ, unpack_k, 0)
    mask_t[...] = mask_n[...].T[0:N, :]
    for j in range(2):
        for ch in range(2):
            kt[ch * N : ch * N + N, j * LP : j * LP + LP] = kn[2 * j + ch].T[0:N, :]
    for load in loads[2:]:
        load.wait()
    high, low = split_f32(kt[...])
    kt[...] = mm(li[...], high) + mm(li[...], low) + mm(lil[...], high)
    for j in range(2):
        columns = jnp.concatenate(
            [kt[0:N, j * LP : j * LP + LP], kt[N : 2 * N, j * LP : j * LP + LP]], axis=1)
        high, low = split_f32(columns)
        gadj[j] = mm(high, rinv[...]) + mm(low, rinv[...]) + mm(high, ril[...])

    for copy in sent[1]:
        copy.wait_recv()

    def unpack_maps(group, carry):
        rows = [got[group * NY + i, 0:32, :].astype(F32) for i in range(NY)]
        at = pl.multiple_of(group * R, 8)
        for j in range(2):
            real, imag = apart(jnp.concatenate([part[10 * j : 10 + 10 * j] for part in rows], axis=0))
            sens[j, 0, pl.ds(at, R), :] = real
            sens[j, 1, pl.ds(at, R), :] = imag
        return carry

    lax.fori_loop(0, NZ, unpack_maps, 0)

    def conjugate_sum(images):
        real, imag = None, None
        for j in range(2):
            a, b = images[j][:, 0:LP], images[j][:, LP : 2 * LP]
            re = sens[j, 0] * a + sens[j, 1] * b
            im = sens[j, 0] * b - sens[j, 1] * a
            real, imag = (re, im) if real is None else (real + re, imag + im)
        return real, imag

    adj[0], adj[1] = conjugate_sum([gadj[0], gadj[1]])

    for step in range(2):
        for j in range(2):
            re = sens[j, 0] * v[0] - sens[j, 1] * v[1]
            im = sens[j, 0] * v[1] + sens[j, 1] * v[0]
            both = mm(jnp.concatenate([re, im], axis=1).astype(BF16), rf[...])
            stage_a[0:N, j * LP : j * LP + LP] = both[:, 0:LP].astype(BF16)
            stage_a[N : 2 * N, j * LP : j * LP + LP] = both[:, LP : 2 * LP].astype(BF16)
        spectrum = mm(lf[...], stage_a[...])
        for ch in range(2):
            for j in range(2):
                stage_b[ch * N : ch * N + N, j * LP : j * LP + LP] = (
                    spectrum[ch * N : ch * N + N, j * LP : j * LP + LP] * mask_t[...]).astype(BF16)
        stage_a[...] = mm(li[...], stage_b[...]).astype(BF16)
        images = []
        for j in range(2):
            images.append(mm(jnp.concatenate(
                [stage_a[0:N, j * LP : j * LP + LP], stage_a[N : 2 * N, j * LP : j * LP + LP]], axis=1), rinv[...]))
        real, imag = conjugate_sum(images)
        real, imag = real - adj[0], imag - adj[1]
        for peer in range(NC):
            rs_out[step, peer] = jnp.concatenate(
                [real[peer * R : peer * R + R, 0:N], imag[peer * R : peer * R + R, 0:N]], axis=0).astype(BF16)
        reduced = to_coil(lambda peer: rs_out.at[step, peer], rs_in.at[step], rs_ss.at[step], rs_rs.at[step])
        rs_in[step, c] = rs_out[step, c]
        for copy in neighbours:
            copy.wait()
        smooth = regular(state, zex0_in if step == 0 else zex1_in, step == 1)
        for copy in reduced:
            copy.wait()
        data = rs_in[step, 0].astype(F32)
        for peer in range(1, NC):
            data = data + rs_in[step, peer].astype(F32)
        state = [
            state[ch][:, 0:N] - STEP_SIZE * (data[ch * R : ch * R + R] + PENALTY * smooth[ch][:, 0:N])
            for ch in range(2)
        ]
        if step == 0:
            chunk = jnp.concatenate(state, axis=0)
            ag_out[...] = chunk.astype(BF16)
            regathered = to_coil(lambda peer: ag_out, ag_in, ag_ss, ag_rs)
            ag_in[c] = ag_out[...]
            zex1_out[1, :, 0:N] = chunk
            neighbours = to_neighbours(1, zex1_out.at[1], zex1_in)
            zero = jnp.zeros((R, LP - N), F32)
            state = [jnp.concatenate([part, zero], axis=1) for part in state]
            for copy in regathered:
                copy.wait()
            for peer in range(NC):
                part = ag_in[peer].astype(F32)
                for ch in range(2):
                    v[ch, peer * R : peer * R + R, 0:N] = part[ch * R : ch * R + R]

    coil_to = s // NY
    slot = lax.rem(s, NY)
    for t in range(4):
        for ch in range(2):
            fin_out[t, ch * 16 : ch * 16 + 10, :] = state[ch][10 * t : 10 * t + 10]

    def final_copy(t):
        return pltpu.make_async_remote_copy(
            src_ref=fin_out.at[t], dst_ref=out.at[slot], send_sem=fin_ss.at[t],
            recv_sem=fin_rs.at[slot], device_id=(4 * c + t, coil_to), device_id_type=MESH)

    for t in range(4):
        is_self = jnp.logical_and(4 * c + t == s, coil_to == c)

        @pl.when(jnp.logical_not(is_self))
        def _():
            final_copy(t).start()

        @pl.when(is_self)
        def _():
            copy = pltpu.make_async_copy(fin_out.at[t], out.at[slot], local_sem.at[1])
            copy.start()
            copy.wait()

    for t in range(4):
        is_self = jnp.logical_and(4 * c + t == s, coil_to == c)

        @pl.when(jnp.logical_not(is_self))
        def _():
            pltpu.make_async_remote_copy(
                src_ref=fin_out.at[t], dst_ref=out.at[t], send_sem=fin_ss.at[t],
                recv_sem=fin_rs.at[t], device_id=(4 * c + t, coil_to), device_id_type=MESH).wait()

    for part in range(2):
        for copy in sent[part]:
            copy.wait_send()


def local(
    noisy_image, noise_draw, block_routes, conv_in, bias_in, norm_gain, conv_mid, bias_mid, conv_out,
    coil_maps, kspace_data, sample_mask,
):
    taps_in = conv_in.astype(F32).reshape(3, 3, 128, 2).transpose(1, 3, 0, 2)
    w_in = jnp.pad(taps_in, ((0, 0), (0, 0), (0, 61), (0, 0))).reshape(384, 128)
    taps_mid = conv_mid.reshape(3, 3, 128, 128).transpose(0, 1, 3, 2).reshape(3, 384, 128)
    w_mid = jnp.concatenate(
        [jnp.pad(taps_mid, ((0, 1), (0, 0), (0, 0))), jnp.pad(taps_mid, ((1, 0), (0, 0), (0, 0)))], axis=2
    ).reshape(1536, 256)
    taps_out = conv_out.astype(F32).reshape(3, 3, 2, 128)[::-1].transpose(3, 1, 2, 0)
    w_out = jnp.pad(taps_out, ((0, 0), (0, 0), (0, 0), (0, 61))).reshape(128, 384)
    tables = [jnp.asarray(table) for table in dft_tables()]
    vmem = pl.BlockSpec(memory_space=pltpu.VMEM)
    hbm = pl.BlockSpec(memory_space=pl.ANY)
    prior, out = pl.pallas_call(
        kernel,
        out_shape=(
            jax.ShapeDtypeStruct((2, 1, R, N), F32),
            jax.ShapeDtypeStruct((4, 32, N), F32),
        ),
        in_specs=[vmem] * 10 + [hbm] * 8,
        out_specs=(vmem, vmem),
        scratch_shapes=[
            pltpu.VMEM((2, 2, NS, 10, N), F32),
            pltpu.VMEM((2, 2, NS, 10, N), F32),
            pltpu.VMEM((2 * N, 2 * N), BF16),
            pltpu.VMEM((2 * N, 2 * N), BF16),
            pltpu.VMEM((2 * N, 2 * N), BF16),
            pltpu.VMEM((2 * LP, 2 * LP), BF16),
            pltpu.VMEM((2 * LP, 2 * LP), BF16),
            pltpu.VMEM((2 * LP, 2 * LP), BF16),
            pltpu.VMEM((NS, 48, 2 * N), BF16),
            pltpu.VMEM((NS, 48, 2 * N), BF16),
            pltpu.VMEM((2, 16, N), F32),
            pltpu.VMEM((2, 16, N), F32),
            pltpu.VMEM((128, LP), F32),
            pltpu.VMEM((LP + 16, 128), F32),
            pltpu.VMEM((N, 384), BF16),
            pltpu.VMEM((N, 44 * LP), BF16),
            pltpu.VMEM((44, N, 128), BF16),
            pltpu.VMEM((N, 384), F32),
            pltpu.VMEM((2 * R, N), F32),
            pltpu.VMEM((NC, 2 * R, N), F32),
            pltpu.VMEM((2, N, LP), F32),
            pltpu.VMEM((2, 2 * R, LP), F32),
            pltpu.VMEM((2, 2 * R, LP), F32),
            pltpu.VMEM((2, 2 * R, LP), F32),
            pltpu.VMEM((4, LP, LP), F32),
            pltpu.VMEM((LP, LP), F32),
            pltpu.VMEM((2 * N, 2 * LP), F32),
            pltpu.VMEM((N, LP), F32),
            pltpu.VMEM((2, N, 2 * LP), F32),
            pltpu.VMEM((2, 2, N, LP), F32),
            pltpu.VMEM((2, N, LP), F32),
            pltpu.VMEM((2 * N, 2 * LP), BF16),
            pltpu.VMEM((2 * N, 2 * LP), BF16),
            pltpu.VMEM((2, NC, 2 * R, N), BF16),
            pltpu.VMEM((2, NC, 2 * R, N), BF16),
            pltpu.VMEM((2 * R, N), BF16),
            pltpu.VMEM((NC, 2 * R, N), BF16),
            pltpu.VMEM((4, 32, N), F32),
            pltpu.SemaphoreType.DMA((8,)),
            pltpu.SemaphoreType.DMA((2,)),
            pltpu.SemaphoreType.DMA((2,)),
            pltpu.SemaphoreType.DMA((2, NS - 1)),
            pltpu.SemaphoreType.DMA((2, NS - 1)),
            pltpu.SemaphoreType.DMA((NC - 1,)),
            pltpu.SemaphoreType.DMA((NC - 1,)),
            pltpu.SemaphoreType.DMA((2, 2)),
            pltpu.SemaphoreType.DMA((2, 2)),
            pltpu.SemaphoreType.DMA((2, NC - 1)),
            pltpu.SemaphoreType.DMA((2, NC - 1)),
            pltpu.SemaphoreType.DMA((NC - 1,)),
            pltpu.SemaphoreType.DMA((NC - 1,)),
            pltpu.SemaphoreType.DMA((4,)),
            pltpu.SemaphoreType.DMA((4,)),
            pltpu.SemaphoreType.DMA((2,)),
        ],
        compiler_params=pltpu.CompilerParams(
            collective_id=0, has_side_effects=True, vmem_limit_bytes=58 * 2**20
        ),
    )(
        noisy_image, noise_draw, block_routes, w_in, bias_in.reshape(1, 128), norm_gain.reshape(1, 128),
        w_mid, bias_mid.reshape(1, 128), w_out, sample_mask, coil_maps, kspace_data, *tables,
    )
    refined = out.reshape(4, 2, 16, N)[:, :, :10].transpose(1, 0, 3, 2)
    return prior, refined


def solution(mesh):
    return jax.shard_map(
        local,
        mesh=mesh,
        in_specs=(
            P(None, "slab", "coil", None),
            P(None, "slab", "coil", None),
            P("slab", None),
            P(), P(), P(), P(), P(), P(),
            P(None, "coil", None, "slab", None),
            P(None, "coil", None, "slab", None),
            P("slab", None),
        ),
        out_specs=(P(None, "slab", "coil", None), P(None, "coil", None, "slab")),
        check_vma=False,
    )
```

```python
import functools
import math

import jax
import jax.numpy as jnp
import numpy as np
from jax import lax
from jax.experimental import pallas as pl
from jax.experimental.pallas import tpu as pltpu
from jax.sharding import PartitionSpec as P

NS, NC, NZ, NY = 32, 8, 8, 4
N = 320
LP = 384
R = 40
STEP_VARIANCE = 1.0 - 0.8 * 0.8
STEP_SCALE = math.sqrt(STEP_VARIANCE)
STEP_SIZE = 0.4
PENALTY = 0.5
SHRINK = 0.3
EPSILON = 1e-05
F32, BF16 = jnp.float32, jnp.bfloat16
MESH = pl.DeviceIdType.MESH
ROWS = 104


def dft_tables():
    index = np.arange(N)
    angle = (index[:, None] * index[None, :] % N) * (2.0 * math.pi / N)
    cosine, sine = np.cos(angle) / math.sqrt(N), np.sin(angle) / math.sqrt(N)

    def left(sign):
        return np.block([[cosine, sign * sine], [-sign * sine, cosine]])

    def right(sign):
        table = np.zeros((2 * LP, 2 * LP))
        table[:N, :N] = table[LP : LP + N, LP : LP + N] = cosine
        table[:N, LP : LP + N] = -sign * sine
        table[LP : LP + N, :N] = sign * sine
        return table

    def split(table):
        import ml_dtypes

        high = table.astype(ml_dtypes.bfloat16)
        return high, (table - high.astype(np.float64)).astype(ml_dtypes.bfloat16)

    left_fwd, left_inv = split(left(1.0))[0], split(left(-1.0))
    right_fwd, right_inv = split(right(1.0))[0], split(right(-1.0))
    return left_fwd, left_inv[0], left_inv[1], right_fwd, right_inv[0], right_inv[1]


def silu(value):
    return value * (0.5 + 0.5 * jnp.tanh(0.5 * value))


def mm(a, b):
    return jnp.dot(a, b, preferred_element_type=F32)


def split_f32(value):
    high = value.astype(BF16)
    return high, (value - high.astype(F32)).astype(BF16)


def kernel(
    noisy, noise, routes, conv_in, b_in, gain, conv_mid, b_mid, conv_out, mask_in,
    maps_hbm, kdata_hbm, lf_hbm, li_hbm, lil_hbm, rf_hbm, ri_hbm, ril_hbm,
    prior, out,
    maps, kdata, lf, li, lil, rf, rinv, ril,
    w_in, w_mid, w_out, w_rows, stage, msg, got, halo_out, halo_in, x_nat, x_t, x3, act3, first, acc,
    ag_out, ag_in, own_out, own_in, v, zex_out, zex_in,
    kn, mk_out, mk_in, mask_t, kt, gadj, sens, adj,
    stage_f, stage_b, rs_out, rs_in, fin_out, fin_in,
    load_sem, halo_ss, halo_rs, a_ss, a_rs, own_ss, own_rs, z_ss, z_rs, mk_ss, mk_rs,
    rs_ss, rs_rs, ag_ss, ag_rs, fin_ss, fin_rs, local_sem,
):
    s, c = lax.axis_index("slab"), lax.axis_index("coil")
    z, y = s // NY, lax.rem(s, NY)
    loads = [
        pltpu.make_async_copy(src, dst, load_sem.at[i])
        for i, (src, dst) in enumerate(
            [(kdata_hbm, kdata), (maps_hbm, maps), (lf_hbm, lf), (li_hbm, li), (lil_hbm, lil),
             (rf_hbm, rf), (ri_hbm, rinv), (ril_hbm, ril)]
        )
    ]
    for load in loads:
        load.start()

    barrier = pltpu.get_barrier_semaphore()
    coil_peers = [lax.rem(c + k, NC) for k in range(1, NC)]
    def slab_to(offset):
        return lax.rem(z + offset // NY, NZ) * NY + lax.rem(y + lax.rem(offset, NY), NY)

    for peer in coil_peers:
        pl.semaphore_signal(barrier, inc=1, device_id=(s, peer), device_id_type=MESH)

    def greet(i, carry):
        pl.semaphore_signal(barrier, inc=1, device_id=(slab_to(i + 1), c), device_id_type=MESH)
        return carry

    lax.fori_loop(0, NS - 1, greet, 0)

    x_nat[...] = jnp.zeros_like(x_nat)
    for ch in range(2):
        rows = noisy[ch, 0].astype(BF16).astype(F32)
        x_nat[ch * 64 + 3 : ch * 64 + 43, 0:N] = rows
        halo_out[0, ch * 8 : ch * 8 + 3, :] = rows[0:3]
        halo_out[1, ch * 8 : ch * 8 + 3, :] = rows[R - 3 : R]

    def beside(real, imag):
        return jnp.concatenate(
            [real[:, 0:256], imag[:, 0:256], jnp.concatenate([real[:, 256:N], imag[:, 256:N]], axis=1)], axis=1
        )

    mask_f = jnp.concatenate([mask_in[...].astype(F32), jnp.zeros((10, LP - N), F32)], axis=1)
    mask_f = pltpu.roll(mask_f, lax.rem(LP - R * c, LP), 1)[:, 0:128]
    lane10 = lax.broadcasted_iota(jnp.int32, (4, 128), 1)
    mask_last = jnp.concatenate([mask_f[8:10], jnp.zeros((2, 128), F32)], axis=0)
    mask_rows = jnp.where(
        lane10 < R, mask_f[0:4],
        jnp.where(lane10 < 2 * R, pltpu.roll(mask_f[4:8], R, 1), pltpu.roll(mask_last, 2 * R, 1)))
    for row in range(4):
        stage[pl.ds(100 + row, NS, stride=ROWS), :] = jnp.broadcast_to(mask_rows[row : row + 1], (NS, 128))

    def pack(part, source):
        loads[part].wait()
        for j in range(2):
            for i in range(10):
                both = beside(source[0, j, i], source[1, j, i])
                for tile in range(5):
                    stage[pl.ds(20 * tile + 10 * j + i, NS, stride=ROWS), :] = both[:, tile * 128 : tile * 128 + 128]

        def narrow(dest, carry):
            msg[part, dest] = stage[pl.ds(pl.multiple_of(dest * ROWS, 8), ROWS), :].astype(BF16)
            return carry

        lax.fori_loop(0, NS, narrow, 0)

    pack(0, kdata)
    pack(1, maps)

    w_in[...] = jnp.zeros_like(w_in)
    w_mid[...] = jnp.zeros_like(w_mid)
    w_rows[...] = jnp.zeros_like(w_rows)
    for a in range(3):
        for b in range(3):
            taps = conv_in[3 * a + b].astype(F32)
            outs = conv_out[3 * a + b].astype(F32)
            for ch in range(2):
                w_in[b * 128 + ch * 64 + a : b * 128 + ch * 64 + a + 1, :] = taps[ch : ch + 1]
                w_rows[b, ch * 64 + 2 - a : ch * 64 + 3 - a, :] = outs[ch : ch + 1]
            middle = conv_mid[3 * a + b].astype(F32).T.astype(BF16)
            for q in range(2):
                at = ((a + q) * 3 + b) * 128
                w_mid[at : at + 128, q * 128 : q * 128 + 128] = middle
    for b in range(3):
        w_out[:, b * 128 : b * 128 + 128] = w_rows[b].T

    pl.semaphore_wait(barrier, NC - 1 + NS - 1)

    up, down = lax.rem(c + NC - 1, NC), lax.rem(c + 1, NC)
    halo = []
    for side, peer in ((0, up), (1, down)):
        copy = pltpu.make_async_remote_copy(
            src_ref=halo_out.at[side], dst_ref=halo_in.at[side], send_sem=halo_ss.at[side],
            recv_sem=halo_rs.at[side], device_id=(s, peer), device_id_type=MESH)
        copy.start()
        halo.append(copy)

    def message(part, offset):
        peer = slab_to(offset)
        return pltpu.make_async_remote_copy(
            src_ref=msg.at[part, peer], dst_ref=got.at[part, s], send_sem=a_ss.at[part, offset - 1],
            recv_sem=a_rs.at[part, offset - 1], device_id=(peer, c), device_id_type=MESH)

    for part in range(2):

        def send(i, carry):
            message(part, i + 1).start()
            return carry

        lax.fori_loop(0, NS - 1, send, 0)
    own_copies = [pltpu.make_async_copy(msg.at[part, s], got.at[part, s], local_sem.at[part]) for part in range(2)]
    for copy in own_copies:
        copy.start()

    x_t[0:8, :] = jnp.zeros((8, 128), F32)

    def build_x3():
        x_t[8 : 8 + LP, :] = x_nat[...].T
        for b in range(3):
            x3[:, b * 128 : b * 128 + 128] = x_t[7 + b : 7 + b + N, :].astype(BF16)

    build_x3()

    column = lax.broadcasted_iota(jnp.int32, (N, 128), 0)

    def shifted(value, offset):
        if offset == 0:
            return value
        if offset < 0:
            return jnp.where(column == 0, 0.0, pltpu.roll(value, 1, 0))
        return jnp.where(column == N - 1, 0.0, pltpu.roll(value, N - 1, 0))

    def inside(row):
        return jnp.where(jnp.logical_and(row >= 0, row < N), 1.0, 0.0).astype(F32)

    def first_pair(pair, carry):
        q = 2 * pair
        weights = jnp.concatenate(
            [pltpu.roll(w_in[...], q, 0), pltpu.roll(w_in[...], q + 1, 0)], axis=1).astype(BF16)
        both = mm(x3[...], weights)
        for half in range(2):
            state = (both[:, half * 128 : half * 128 + 128] + b_in[...]).astype(BF16)
            first[q + half] = state
            state = state.astype(F32)
            scale = lax.rsqrt(jnp.mean(state * state, axis=-1, keepdims=True) + EPSILON)
            active = silu(state * scale * gain[...]) * inside(c * R - 2 + q + half)
            for b in range(3):
                at = pl.multiple_of((q + half) * LP + b * 128, 128)
                act3[:, pl.ds(at, 128)] = shifted(active, b - 1).astype(BF16)
        return carry

    lax.fori_loop(2, 20, first_pair, 0)
    for copy in halo:
        copy.wait()
    for ch in range(2):
        above = jnp.where(c > 0, halo_in[1, ch * 8 : ch * 8 + 3, :], 0.0)
        below = jnp.where(c < NC - 1, halo_in[0, ch * 8 : ch * 8 + 3, :], 0.0)
        x_nat[ch * 64 : ch * 64 + 3, 0:N] = above
        x_nat[ch * 64 + 43 : ch * 64 + 46, 0:N] = below
    build_x3()
    lax.fori_loop(0, 2, first_pair, 0)
    lax.fori_loop(20, 22, first_pair, 0)

    acc[...] = jnp.zeros_like(acc)

    def second_pair(pair, carry):
        p = 2 * pair
        both = mm(act3[:, pl.ds(pl.multiple_of(p * LP, 128), 4 * LP)], w_mid[...])
        halves, weights = [], []
        for half in range(2):
            second = first[p + half + 1].astype(F32) + both[:, half * 128 : half * 128 + 128] + b_mid[...]
            second = second.astype(BF16).astype(F32)
            halves.append((silu(second) * inside(c * R - 1 + p + half)).astype(BF16))
            weights.append(jnp.concatenate(
                [pltpu.roll(w_out[:, b * 128 : b * 128 + 128], lax.rem(p + half + 126, 128), 1) for b in range(3)],
                axis=1))
        acc[...] += mm(jnp.concatenate(halves, axis=1), jnp.concatenate(weights, axis=0).astype(BF16))
        return carry

    lax.fori_loop(0, 21, second_pair, 0)

    score_t = shifted(acc[:, 0:128], -1) + acc[:, 128:256] + shifted(acc[:, 256:384], 1)
    x_t[0:N, :] = score_t
    score = x_t[0:LP, :].T
    block = lax.broadcasted_iota(jnp.int32, (R, 40), 1)
    block_of_row = c * 5 + lax.broadcasted_iota(jnp.int32, (R, 40), 0) // 8
    routed = jnp.where(routes[...] >= 0, 1.0, 0.0).astype(F32)
    keep = jnp.sum(jnp.where(block == block_of_row, jnp.broadcast_to(routed, (R, 40)), 0.0), axis=1, keepdims=True)
    stepped_parts = []
    for ch in range(2):
        value = score[ch * 64 : ch * 64 + R, 0:N].astype(BF16).astype(F32) * keep
        stepped = noisy[ch, 0] + STEP_VARIANCE * value + STEP_SCALE * noise[ch, 0]
        prior[ch, 0] = stepped
        x_nat[ch * 64 : ch * 64 + R, 0:N] = stepped
        stepped_parts.append(stepped)
    ag_out[0] = beside(stepped_parts[0], stepped_parts[1]).astype(BF16)

    def to_coil(src_of, dst, send_sems, recv_sems):
        copies = []
        for i, peer in enumerate(coil_peers):
            copy = pltpu.make_async_remote_copy(
                src_ref=src_of(peer), dst_ref=dst.at[c], send_sem=send_sems.at[i],
                recv_sem=recv_sems.at[i], device_id=(s, peer), device_id_type=MESH)
            copy.start()
            copies.append(copy)
        return copies

    gathered = to_coil(lambda peer: ag_out.at[0], ag_in.at[0], ag_ss.at[0], ag_rs.at[0])
    ag_in[0, c] = ag_out[0]
    own_out[...] = x_nat[...].T[0:N].reshape(NC, R, 128)
    chunked = to_coil(lambda peer: own_out.at[peer], own_in, own_ss, own_rs)
    own_in[c] = own_out[c]

    def to_neighbours(number):
        copies = []
        for side, peer in ((0, lax.rem(s + NS - 1, NS)), (1, lax.rem(s + 1, NS))):
            copy = pltpu.make_async_remote_copy(
                src_ref=zex_out.at[number], dst_ref=zex_in.at[number, side], send_sem=z_ss.at[number, side],
                recv_sem=z_rs.at[number, side], device_id=(peer, c), device_id_type=MESH)
            copy.start()
            copies.append(copy)
        return copies

    lane = lax.broadcasted_iota(jnp.int32, (R, 128), 1)
    lanes = lax.broadcasted_iota(jnp.int32, (R, LP), 1)

    def apart(tiles):
        zero = jnp.zeros_like(tiles[4])
        real_tail = jnp.where(lane < 64, tiles[4], zero)
        imag_tail = jnp.where(lane < 64, pltpu.roll(tiles[4], 64, 1), zero)
        return (jnp.concatenate([tiles[0], tiles[1], real_tail], axis=1),
                jnp.concatenate([tiles[2], tiles[3], imag_tail], axis=1))

    def apart_rows(rows):
        rows = rows.astype(F32)
        return apart([rows[:, k * 128 : k * 128 + 128] for k in range(5)])

    for copy in chunked:
        copy.wait()
    state = []
    for ch in range(2):
        total = jnp.zeros((R, LP), F32)
        for peer in range(NC):
            piece = own_in[peer]
            piece = jnp.concatenate([piece if ch == 0 else pltpu.roll(piece, 64, 1)] + [jnp.zeros((R, 256), F32)], axis=1)
            piece = piece if peer == 0 else pltpu.roll(piece, R * peer, 1)
            total = jnp.where(jnp.logical_and(lanes >= R * peer, lanes < R * peer + R), piece, total)
        state.append(total)
        zex_out[0, ch * R : ch * R + R, :] = total
    neighbours = to_neighbours(0)
    for copy in gathered:
        copy.wait()
    kn[...] = jnp.zeros_like(kn)
    for peer in range(NC):
        real, imag = apart_rows(ag_in[0, peer])
        kn[0, peer * R : peer * R + R, :] = real
        kn[1, peer * R : peer * R + R, :] = imag
    for ch in range(2):
        v[ch] = kn[ch].T[0:N, :]

    def regular(state, received, clip):
        result = []
        for ch in range(2):
            behind = received[1, ch * R : ch * R + R, :]
            ahead = received[0, ch * R : ch * R + R, :]
            low, high = state[ch] - behind, ahead - state[ch]
            if clip:
                low, high = 2.0 * jnp.clip(low, -SHRINK, SHRINK), 2.0 * jnp.clip(high, -SHRINK, SHRINK)
            result.append(jnp.where(s > 0, low, 0.0) - jnp.where(s < NS - 1, high, 0.0))
        return result

    mask_t[...] = jnp.zeros_like(mask_t)
    kn[...] = jnp.zeros_like(kn)

    def arrived(part, group_offset):
        for dy in range(NY):
            message(part, group_offset * NY + dy).wait_recv()

    def unpack(part, group, store):
        rows = [got[part, group * NY + i].astype(F32) for i in range(NY)]
        at = pl.multiple_of(group * R, 8)
        for j in range(2):
            tiles = [
                jnp.concatenate([rows[i][20 * k + 10 * j : 20 * k + 10 * j + 10] for i in range(NY)], axis=0)
                for k in range(5)
            ]
            store(j, at, apart(tiles))
        return rows, at

    def store_k(j, at, pair):
        kn[2 * j, pl.ds(at, R), :] = pair[0]
        kn[2 * j + 1, pl.ds(at, R), :] = pair[1]

    def unpack_k(group):
        rows, at = unpack(0, group, store_k)
        marks = []
        for i in range(NY):
            part = rows[i][100:104]
            marks += [part, pltpu.roll(part, 128 - R, 1), pltpu.roll(part, 128 - 2 * R, 1)[0:2]]
        x_t[pl.ds(at, R), :] = jnp.concatenate(marks, axis=0)

    def first_group(part):
        own_copies[part].wait()
        for dy in range(1, NY):
            message(part, dy).wait_recv()

    first_group(0)
    unpack_k(z)

    def next_k(dz, carry):
        arrived(0, dz)
        unpack_k(lax.rem(z + NZ - dz, NZ))
        return carry

    lax.fori_loop(1, NZ, next_k, 0)
    mk_out[...] = x_t[0:LP, :].T[0:R, 0:N].astype(BF16)
    masks = to_coil(lambda peer: mk_out, mk_in, mk_ss, mk_rs)
    mk_in[c] = mk_out[...]
    for j in range(2):
        for ch in range(2):
            kt[ch * N : ch * N + N, j * LP : j * LP + LP] = kn[2 * j + ch].T[0:N, :]
    for copy in masks:
        copy.wait()
    for peer in range(NC):
        mask_t[peer * R : peer * R + R, 0:N] = mk_in[peer].astype(F32)
    for ch in range(2):
        for j in range(2):
            kt[ch * N : ch * N + N, j * LP : j * LP + LP] *= mask_t[...]
    for load in loads[2:]:
        load.wait()
    high, low = split_f32(kt[...])
    kt[...] = mm(li[...], high) + mm(li[...], low) + mm(lil[...], high)
    for j in range(2):
        columns = jnp.concatenate(
            [kt[0:N, j * LP : j * LP + LP], kt[N : 2 * N, j * LP : j * LP + LP]], axis=1)
        high, low = split_f32(columns)
        gadj[j] = mm(high, rinv[...]) + mm(low, rinv[...]) + mm(high, ril[...])

    def store_maps(j, at, pair):
        sens[j, 0, pl.ds(at, R), :] = pair[0]
        sens[j, 1, pl.ds(at, R), :] = pair[1]

    first_group(1)
    unpack(1, z, store_maps)

    def next_maps(dz, carry):
        arrived(1, dz)
        unpack(1, lax.rem(z + NZ - dz, NZ), store_maps)
        return carry

    lax.fori_loop(1, NZ, next_maps, 0)

    def conjugate_sum(rows, images):
        real, imag = None, None
        for j in range(2):
            a, b = images[j][:, 0:LP], images[j][:, LP : 2 * LP]
            re = sens[j, 0, rows] * a + sens[j, 1, rows] * b
            im = sens[j, 0, rows] * b - sens[j, 1, rows] * a
            real, imag = (re, im) if real is None else (real + re, imag + im)
        return real, imag

    adj[0], adj[1] = conjugate_sum(pl.ds(0, N), [gadj[0], gadj[1]])

    def forward_rows(at, vr, vi):
        rows = pl.ds(at, R)
        for j in range(2):
            mr, mi = sens[j, 0, rows], sens[j, 1, rows]
            both = mm(jnp.concatenate([mr * vr - mi * vi, mr * vi + mi * vr], axis=1).astype(BF16), rf[...])
            for ch in range(2):
                part = both[:, ch * LP : ch * LP + LP]
                stage_f[pl.ds(ch * N + at, R), j * LP : j * LP + LP] = part

    def reduce_to(step, peer):
        rows = pl.ds(pl.multiple_of(peer * R, 8), R)
        images = []
        for j in range(2):
            columns = jnp.concatenate(
                [stage_f[rows, j * LP : j * LP + LP],
                 stage_f[pl.ds(pl.multiple_of(N + peer * R, 8), R), j * LP : j * LP + LP]], axis=1)
            images.append(mm(columns.astype(BF16), rinv[...]))
        real, imag = conjugate_sum(rows, images)
        rs_out[step, peer] = beside((real - adj[0, rows])[:, 0:N], (imag - adj[1, rows])[:, 0:N]).astype(BF16)

    for step in range(2):
        if step == 0:
            for peer in range(NC):
                forward_rows(peer * R, v[0, peer * R : peer * R + R, :], v[1, peer * R : peer * R + R, :])
        else:
            forward_rows(pl.multiple_of(c * R, 8), *apart_rows(ag_out[1]))
            for i, copy in enumerate(regathered):
                copy.wait_recv()
                sender = lax.rem(c + NC - 1 - i, NC)
                forward_rows(pl.multiple_of(sender * R, 8), *apart_rows(ag_in[1, sender]))
        spectrum = mm(lf[...], stage_f[...].astype(BF16))
        for ch in range(2):
            for j in range(2):
                stage_b[ch * N : ch * N + N, j * LP : j * LP + LP] = (
                    spectrum[ch * N : ch * N + N, j * LP : j * LP + LP] * mask_t[...]).astype(BF16)
        stage_f[...] = mm(li[...], stage_b[...])
        reduced = []
        for i, peer in enumerate(coil_peers):
            reduce_to(step, peer)
            copy = pltpu.make_async_remote_copy(
                src_ref=rs_out.at[step, peer], dst_ref=rs_in.at[step, c], send_sem=rs_ss.at[step, i],
                recv_sem=rs_rs.at[step, i], device_id=(s, peer), device_id_type=MESH)
            copy.start()
            reduced.append(copy)
        reduce_to(step, c)
        for copy in neighbours:
            copy.wait()
        smooth = regular(state, zex_in.at[step], step == 1)
        data = rs_out[step, c].astype(F32)
        for i, copy in enumerate(reduced):
            copy.wait()
            data = data + rs_in[step, lax.rem(c + NC - 1 - i, NC)].astype(F32)
        data = apart([data[:, k * 128 : k * 128 + 128] for k in range(5)])
        state = [state[ch] - STEP_SIZE * (data[ch] + PENALTY * smooth[ch]) for ch in range(2)]
        if step == 0:
            ag_out[1] = beside(state[0][:, 0:N], state[1][:, 0:N]).astype(BF16)
            regathered = to_coil(lambda peer: ag_out.at[1], ag_in.at[1], ag_ss.at[1], ag_rs.at[1])
            zex_out[1] = jnp.concatenate(state, axis=0)
            neighbours = to_neighbours(1)

    coil_to = s // NY
    slot = lax.rem(s, NY)
    result = beside(state[0][:, 0:N], state[1][:, 0:N])

    def final_copy(t, at):
        return pltpu.make_async_remote_copy(
            src_ref=fin_out.at[t], dst_ref=fin_in.at[at], send_sem=fin_ss.at[t],
            recv_sem=fin_rs.at[at], device_id=(4 * c + t, coil_to), device_id_type=MESH)

    for t in range(4):
        is_self = jnp.logical_and(4 * c + t == s, coil_to == c)
        for k in range(5):
            fin_out[t, 10 * k : 10 * k + 10, :] = result[10 * t : 10 * t + 10, k * 128 : k * 128 + 128]

        @pl.when(jnp.logical_not(is_self))
        def _():
            final_copy(t, slot).start()

        @pl.when(is_self)
        def _():
            copy = pltpu.make_async_copy(fin_out.at[t], fin_in.at[slot], local_sem.at[2])
            copy.start()
            copy.wait()

    for copy in regathered:
        copy.wait_send()
    for part in range(2):

        def sent(i, carry):
            message(part, i + 1).wait_send()
            return carry

        lax.fori_loop(0, NS - 1, sent, 0)

    for t in range(4):
        is_self = jnp.logical_and(4 * c + t == s, coil_to == c)

        @pl.when(jnp.logical_not(is_self))
        def _():
            final_copy(t, t).wait()

        rows = fin_in[t]
        tiles = [rows[10 * k : 10 * k + 10] for k in range(5)]
        tiles[4] = tiles[4][:, 0:64], tiles[4][:, 64:128]
        for ch in range(2):
            out[ch, :, t, :] = jnp.concatenate([tiles[2 * ch], tiles[2 * ch + 1], tiles[4][ch]], axis=1)


def local(
    noisy_image, noise_draw, block_routes, conv_in, bias_in, norm_gain, conv_mid, bias_mid, conv_out,
    coil_maps, kspace_data, sample_mask,
):
    tables = [jnp.asarray(table) for table in dft_tables()]
    vmem = pl.BlockSpec(memory_space=pltpu.VMEM)
    hbm = pl.BlockSpec(memory_space=pl.ANY)
    prior, out = pl.pallas_call(
        kernel,
        out_shape=(
            jax.ShapeDtypeStruct((2, 1, R, N), F32),
            jax.ShapeDtypeStruct((2, 10, 4, N), F32),
        ),
        in_specs=[vmem] * 10 + [hbm] * 8,
        out_specs=(vmem, vmem),
        scratch_shapes=[
            pltpu.VMEM((2, 2, 10, NS, N), F32),
            pltpu.VMEM((2, 2, 10, NS, N), F32),
            pltpu.VMEM((2 * N, 2 * N), BF16),
            pltpu.VMEM((2 * N, 2 * N), BF16),
            pltpu.VMEM((2 * N, 2 * N), BF16),
            pltpu.VMEM((2 * LP, 2 * LP), BF16),
            pltpu.VMEM((2 * LP, 2 * LP), BF16),
            pltpu.VMEM((2 * LP, 2 * LP), BF16),
            pltpu.VMEM((384, 128), F32),
            pltpu.VMEM((1536, 256), BF16),
            pltpu.VMEM((128, 384), F32),
            pltpu.VMEM((3, 128, 128), F32),
            pltpu.VMEM((NS * ROWS, 128), F32),
            pltpu.VMEM((2, NS, ROWS, 128), BF16),
            pltpu.VMEM((2, NS, ROWS, 128), BF16),
            pltpu.VMEM((2, 16, N), F32),
            pltpu.VMEM((2, 16, N), F32),
            pltpu.VMEM((128, LP), F32),
            pltpu.VMEM((LP + 16, 128), F32),
            pltpu.VMEM((N, 384), BF16),
            pltpu.VMEM((N, 44 * LP), BF16),
            pltpu.VMEM((44, N, 128), BF16),
            pltpu.VMEM((N, 384), F32),
            pltpu.VMEM((2, R, 2 * N), BF16),
            pltpu.VMEM((2, NC, R, 2 * N), BF16),
            pltpu.VMEM((NC, R, 128), F32),
            pltpu.VMEM((NC, R, 128), F32),
            pltpu.VMEM((2, N, LP), F32),
            pltpu.VMEM((2, 2 * R, LP), F32),
            pltpu.VMEM((2, 2, 2 * R, LP), F32),
            pltpu.VMEM((4, LP, LP), F32),
            pltpu.VMEM((R, N), BF16),
            pltpu.VMEM((NC, R, N), BF16),
            pltpu.VMEM((N, LP), F32),
            pltpu.VMEM((2 * N, 2 * LP), F32),
            pltpu.VMEM((2, N, 2 * LP), F32),
            pltpu.VMEM((2, 2, N, LP), F32),
            pltpu.VMEM((2, N, LP), F32),
            pltpu.VMEM((2 * N, 2 * LP), F32),
            pltpu.VMEM((2 * N, 2 * LP), BF16),
            pltpu.VMEM((2, NC, R, 2 * N), BF16),
            pltpu.VMEM((2, NC, R, 2 * N), BF16),
            pltpu.VMEM((4, 56, 128), F32),
            pltpu.VMEM((4, 56, 128), F32),
            pltpu.SemaphoreType.DMA((8,)),
            pltpu.SemaphoreType.DMA((2,)),
            pltpu.SemaphoreType.DMA((2,)),
            pltpu.SemaphoreType.DMA((2, NS - 1)),
            pltpu.SemaphoreType.DMA((2, NS - 1)),
            pltpu.SemaphoreType.DMA((NC - 1,)),
            pltpu.SemaphoreType.DMA((NC - 1,)),
            pltpu.SemaphoreType.DMA((2, 2)),
            pltpu.SemaphoreType.DMA((2, 2)),
            pltpu.SemaphoreType.DMA((NC - 1,)),
            pltpu.SemaphoreType.DMA((NC - 1,)),
            pltpu.SemaphoreType.DMA((2, NC - 1)),
            pltpu.SemaphoreType.DMA((2, NC - 1)),
            pltpu.SemaphoreType.DMA((2, NC - 1)),
            pltpu.SemaphoreType.DMA((2, NC - 1)),
            pltpu.SemaphoreType.DMA((4,)),
            pltpu.SemaphoreType.DMA((4,)),
            pltpu.SemaphoreType.DMA((3,)),
        ],
        compiler_params=pltpu.CompilerParams(
            collective_id=0, has_side_effects=True, vmem_limit_bytes=58 * 2**20
        ),
    )(
        noisy_image, noise_draw, block_routes, conv_in.transpose(0, 2, 1), bias_in.reshape(1, 128),
        norm_gain.reshape(1, 128), conv_mid, bias_mid.reshape(1, 128), conv_out, sample_mask,
        coil_maps.transpose(0, 1, 3, 2, 4), kspace_data.transpose(0, 1, 3, 2, 4), *tables,
    )
    refined = out.transpose(0, 2, 3, 1)
    return prior, refined


def solution(mesh):
    return jax.shard_map(
        local,
        mesh=mesh,
        in_specs=(
            P(None, "slab", "coil", None),
            P(None, "slab", "coil", None),
            P("slab", None),
            P(), P(), P(), P(), P(), P(),
            P(None, "coil", None, "slab", None),
            P(None, "coil", None, "slab", None),
            P("slab", None),
        ),
        out_specs=(P(None, "slab", "coil", None), P(None, "coil", None, "slab")),
        check_vma=False,
    )
```

```python
import functools
import math

import jax
import jax.numpy as jnp
import numpy as np
from jax import lax
from jax.experimental import pallas as pl
from jax.experimental.pallas import tpu as pltpu
from jax.sharding import PartitionSpec as P

NS, NC, NZ, NY = 32, 8, 8, 4
N = 320
LP = 384
R = 40
STEP_VARIANCE = 1.0 - 0.8 * 0.8
STEP_SCALE = math.sqrt(STEP_VARIANCE)
STEP_SIZE = 0.4
PENALTY = 0.5
SHRINK = 0.3
EPSILON = 1e-05
F32, BF16 = jnp.float32, jnp.bfloat16
MESH = pl.DeviceIdType.MESH
ROWS = 104


def dft_tables():
    index = np.arange(N)
    angle = (index[:, None] * index[None, :] % N) * (2.0 * math.pi / N)
    cosine, sine = np.cos(angle) / math.sqrt(N), np.sin(angle) / math.sqrt(N)

    def left(sign):
        return np.block([[cosine, sign * sine], [-sign * sine, cosine]])

    def right(sign):
        table = np.zeros((2 * LP, 2 * LP))
        table[:N, :N] = table[LP : LP + N, LP : LP + N] = cosine
        table[:N, LP : LP + N] = -sign * sine
        table[LP : LP + N, :N] = sign * sine
        return table

    def split(table):
        import ml_dtypes

        high = table.astype(ml_dtypes.bfloat16)
        return high, (table - high.astype(np.float64)).astype(ml_dtypes.bfloat16)

    left_fwd, left_inv = split(left(1.0))[0], split(left(-1.0))
    right_fwd, right_inv = split(right(1.0))[0], split(right(-1.0))
    return left_fwd, left_inv[0], left_inv[1], right_fwd, right_inv[0], right_inv[1]


def silu(value):
    return value * (0.5 + 0.5 * jnp.tanh(0.5 * value))


def mm(a, b):
    return jnp.dot(a, b, preferred_element_type=F32)


def split_f32(value):
    high = value.astype(BF16)
    return high, (value - high.astype(F32)).astype(BF16)


def kernel(
    noisy, noise, routes, conv_in, b_in, gain, conv_mid, b_mid, conv_out, mask_in,
    maps_hbm, kdata_hbm, lf_hbm, li_hbm, lil_hbm, rf_hbm, ri_hbm, ril_hbm,
    prior, out,
    maps, kdata, lf, li, lil, rf, rinv, ril,
    w_in, w_mid, w_out, w_rows, stage, msg, got, halo_out, halo_in, x_nat, x_t, x3, act3, first, acc,
    ag_out, ag_in, own_out, own_in, v, zex_out, zex_in,
    kn, mk_out, mk_in, mask_t, kt, gadj, sens, adj,
    stage_f, stage_b, rs_out, rs_in, fin_out, fin_in,
    load_sem, halo_ss, halo_rs, a_ss, a_rs, own_ss, own_rs, z_ss, z_rs, mk_ss, mk_rs,
    rs_ss, rs_rs, ag_ss, ag_rs, fin_ss, fin_rs, local_sem,
):
    s, c = lax.axis_index("slab"), lax.axis_index("coil")
    z, y = s // NY, lax.rem(s, NY)
    loads = [
        pltpu.make_async_copy(src, dst, load_sem.at[i])
        for i, (src, dst) in enumerate(
            [(kdata_hbm, kdata), (maps_hbm, maps), (lf_hbm, lf), (li_hbm, li), (lil_hbm, lil),
             (rf_hbm, rf), (ri_hbm, rinv), (ril_hbm, ril)]
        )
    ]
    for load in loads:
        load.start()

    barrier = pltpu.get_barrier_semaphore()
    coil_peers = [lax.rem(c + k, NC) for k in range(1, NC)]
    def slab_to(offset):
        return lax.rem(z + offset // NY, NZ) * NY + lax.rem(y + lax.rem(offset, NY), NY)

    for peer in coil_peers:
        pl.semaphore_signal(barrier, inc=1, device_id=(s, peer), device_id_type=MESH)

    def greet(i, carry):
        pl.semaphore_signal(barrier, inc=1, device_id=(slab_to(i + 1), c), device_id_type=MESH)
        return carry

    lax.fori_loop(0, NS - 1, greet, 0)

    x_nat[...] = jnp.zeros_like(x_nat)
    for ch in range(2):
        rows = noisy[ch, 0].astype(BF16).astype(F32)
        x_nat[ch * 64 + 3 : ch * 64 + 43, 0:N] = rows
        halo_out[0, ch * 8 : ch * 8 + 3, :] = rows[0:3]
        halo_out[1, ch * 8 : ch * 8 + 3, :] = rows[R - 3 : R]

    def beside(real, imag):
        return jnp.concatenate(
            [real[:, 0:256], imag[:, 0:256], jnp.concatenate([real[:, 256:N], imag[:, 256:N]], axis=1)], axis=1
        )

    mask_f = jnp.concatenate([mask_in[...].astype(F32), jnp.zeros((10, LP - N), F32)], axis=1)
    mask_f = pltpu.roll(mask_f, lax.rem(LP - R * c, LP), 1)[:, 0:128]
    lane10 = lax.broadcasted_iota(jnp.int32, (4, 128), 1)
    mask_last = jnp.concatenate([mask_f[8:10], jnp.zeros((2, 128), F32)], axis=0)
    mask_rows = jnp.where(
        lane10 < R, mask_f[0:4],
        jnp.where(lane10 < 2 * R, pltpu.roll(mask_f[4:8], R, 1), pltpu.roll(mask_last, 2 * R, 1)))
    for row in range(4):
        stage[pl.ds(100 + row, NS, stride=ROWS), :] = jnp.broadcast_to(mask_rows[row : row + 1], (NS, 128))

    def pack(part, source):
        loads[part].wait()
        for j in range(2):
            for i in range(10):
                both = beside(source[0, j, i], source[1, j, i])
                for tile in range(5):
                    stage[pl.ds(20 * tile + 10 * j + i, NS, stride=ROWS), :] = both[:, tile * 128 : tile * 128 + 128]

        def narrow(dest, carry):
            msg[part, dest] = stage[pl.ds(pl.multiple_of(dest * ROWS, 8), ROWS), :].astype(BF16)
            return carry

        lax.fori_loop(0, NS, narrow, 0)

    pack(0, kdata)
    pack(1, maps)

    w_in[...] = jnp.zeros_like(w_in)
    w_mid[...] = jnp.zeros_like(w_mid)
    w_rows[...] = jnp.zeros_like(w_rows)
    for a in range(3):
        for b in range(3):
            taps = conv_in[3 * a + b].astype(F32)
            outs = conv_out[3 * a + b].astype(F32)
            for ch in range(2):
                w_in[b * 128 + ch * 64 + a : b * 128 + ch * 64 + a + 1, :] = taps[ch : ch + 1]
                w_rows[b, ch * 64 + 2 - a : ch * 64 + 3 - a, :] = outs[ch : ch + 1]
            middle = conv_mid[3 * a + b].astype(F32).T.astype(BF16)
            for q in range(2):
                at = ((a + q) * 3 + b) * 128
                w_mid[at : at + 128, q * 128 : q * 128 + 128] = middle
    for b in range(3):
        w_out[:, b * 128 : b * 128 + 128] = w_rows[b].T

    pl.semaphore_wait(barrier, NC - 1 + NS - 1)

    up, down = lax.rem(c + NC - 1, NC), lax.rem(c + 1, NC)
    halo = []
    for side, peer in ((0, up), (1, down)):
        copy = pltpu.make_async_remote_copy(
            src_ref=halo_out.at[side], dst_ref=halo_in.at[side], send_sem=halo_ss.at[side],
            recv_sem=halo_rs.at[side], device_id=(s, peer), device_id_type=MESH)
        copy.start()
        halo.append(copy)

    def message(part, offset):
        peer = slab_to(offset)
        return pltpu.make_async_remote_copy(
            src_ref=msg.at[part, peer], dst_ref=got.at[part, s], send_sem=a_ss.at[part, offset - 1],
            recv_sem=a_rs.at[part, offset - 1], device_id=(peer, c), device_id_type=MESH)

    for part in range(2):

        def send(i, carry):
            message(part, i + 1).start()
            return carry

        lax.fori_loop(0, NS - 1, send, 0)
    own_copies = [pltpu.make_async_copy(msg.at[part, s], got.at[part, s], local_sem.at[part]) for part in range(2)]
    for copy in own_copies:
        copy.start()

    x_t[0:8, :] = jnp.zeros((8, 128), F32)

    def build_x3():
        x_t[8 : 8 + LP, :] = x_nat[...].T
        for b in range(3):
            x3[:, b * 128 : b * 128 + 128] = x_t[7 + b : 7 + b + N, :].astype(BF16)

    build_x3()

    column = lax.broadcasted_iota(jnp.int32, (N, 128), 0)

    def shifted(value, offset):
        if offset == 0:
            return value
        if offset < 0:
            return jnp.where(column == 0, 0.0, pltpu.roll(value, 1, 0))
        return jnp.where(column == N - 1, 0.0, pltpu.roll(value, N - 1, 0))

    def inside(row):
        return jnp.where(jnp.logical_and(row >= 0, row < N), 1.0, 0.0).astype(F32)

    def first_pair(pair, carry):
        q = 2 * pair
        weights = jnp.concatenate(
            [pltpu.roll(w_in[...], q, 0), pltpu.roll(w_in[...], q + 1, 0)], axis=1).astype(BF16)
        both = mm(x3[...], weights)
        for half in range(2):
            state = (both[:, half * 128 : half * 128 + 128] + b_in[...]).astype(BF16)
            first[q + half] = state
            state = state.astype(F32)
            scale = lax.rsqrt(jnp.mean(state * state, axis=-1, keepdims=True) + EPSILON)
            active = silu(state * scale * gain[...]) * inside(c * R - 2 + q + half)
            for b in range(3):
                at = pl.multiple_of((q + half) * LP + b * 128, 128)
                act3[:, pl.ds(at, 128)] = shifted(active, b - 1).astype(BF16)
        return carry

    lax.fori_loop(2, 20, first_pair, 0)
    for copy in halo:
        copy.wait()
    for ch in range(2):
        above = jnp.where(c > 0, halo_in[1, ch * 8 : ch * 8 + 3, :], 0.0)
        below = jnp.where(c < NC - 1, halo_in[0, ch * 8 : ch * 8 + 3, :], 0.0)
        x_nat[ch * 64 : ch * 64 + 3, 0:N] = above
        x_nat[ch * 64 + 43 : ch * 64 + 46, 0:N] = below
    build_x3()
    lax.fori_loop(0, 2, first_pair, 0)
    lax.fori_loop(20, 22, first_pair, 0)

    acc[...] = jnp.zeros_like(acc)

    def second_pair(pair, carry):
        p = 2 * pair
        both = mm(act3[:, pl.ds(pl.multiple_of(p * LP, 128), 4 * LP)], w_mid[...])
        halves, weights = [], []
        for half in range(2):
            second = first[p + half + 1].astype(F32) + both[:, half * 128 : half * 128 + 128] + b_mid[...]
            second = second.astype(BF16).astype(F32)
            halves.append((silu(second) * inside(c * R - 1 + p + half)).astype(BF16))
            weights.append(jnp.concatenate(
                [pltpu.roll(w_out[:, b * 128 : b * 128 + 128], lax.rem(p + half + 126, 128), 1) for b in range(3)],
                axis=1))
        acc[...] += mm(jnp.concatenate(halves, axis=1), jnp.concatenate(weights, axis=0).astype(BF16))
        return carry

    lax.fori_loop(0, 21, second_pair, 0)

    score_t = shifted(acc[:, 0:128], -1) + acc[:, 128:256] + shifted(acc[:, 256:384], 1)
    x_t[0:N, :] = score_t
    score = x_t[0:LP, :].T
    block = lax.broadcasted_iota(jnp.int32, (R, 40), 1)
    block_of_row = c * 5 + lax.broadcasted_iota(jnp.int32, (R, 40), 0) // 8
    routed = jnp.where(routes[...] >= 0, 1.0, 0.0).astype(F32)
    keep = jnp.sum(jnp.where(block == block_of_row, jnp.broadcast_to(routed, (R, 40)), 0.0), axis=1, keepdims=True)
    stepped_parts = []
    for ch in range(2):
        value = score[ch * 64 : ch * 64 + R, 0:N].astype(BF16).astype(F32) * keep
        stepped = noisy[ch, 0] + STEP_VARIANCE * value + STEP_SCALE * noise[ch, 0]
        prior[ch, 0] = stepped
        x_nat[ch * 64 : ch * 64 + R, 0:N] = stepped
        stepped_parts.append(stepped)
    ag_out[0] = beside(stepped_parts[0], stepped_parts[1]).astype(BF16)

    def to_coil(src_of, dst, send_sems, recv_sems):
        copies = []
        for i, peer in enumerate(coil_peers):
            copy = pltpu.make_async_remote_copy(
                src_ref=src_of(peer), dst_ref=dst.at[c], send_sem=send_sems.at[i],
                recv_sem=recv_sems.at[i], device_id=(s, peer), device_id_type=MESH)
            copy.start()
            copies.append(copy)
        return copies

    gathered = to_coil(lambda peer: ag_out.at[0], ag_in.at[0], ag_ss.at[0], ag_rs.at[0])
    ag_in[0, c] = ag_out[0]
    own_out[...] = x_nat[...].T[0:N].reshape(NC, R, 128)
    chunked = to_coil(lambda peer: own_out.at[peer], own_in, own_ss, own_rs)
    own_in[c] = own_out[c]

    def to_neighbours(number):
        copies = []
        for side, peer in ((0, lax.rem(s + NS - 1, NS)), (1, lax.rem(s + 1, NS))):
            copy = pltpu.make_async_remote_copy(
                src_ref=zex_out.at[number], dst_ref=zex_in.at[number, side], send_sem=z_ss.at[number, side],
                recv_sem=z_rs.at[number, side], device_id=(peer, c), device_id_type=MESH)
            copy.start()
            copies.append(copy)
        return copies

    lane = lax.broadcasted_iota(jnp.int32, (R, 128), 1)
    lanes = lax.broadcasted_iota(jnp.int32, (R, LP), 1)

    def apart(tiles):
        zero = jnp.zeros_like(tiles[4])
        real_tail = jnp.where(lane < 64, tiles[4], zero)
        imag_tail = jnp.where(lane < 64, pltpu.roll(tiles[4], 64, 1), zero)
        return (jnp.concatenate([tiles[0], tiles[1], real_tail], axis=1),
                jnp.concatenate([tiles[2], tiles[3], imag_tail], axis=1))

    def apart_rows(rows):
        rows = rows.astype(F32)
        return apart([rows[:, k * 128 : k * 128 + 128] for k in range(5)])

    def regular(state, received, clip):
        result = []
        for ch in range(2):
            behind = received[1, ch * R : ch * R + R, :]
            ahead = received[0, ch * R : ch * R + R, :]
            low, high = state[ch] - behind, ahead - state[ch]
            if clip:
                low, high = 2.0 * jnp.clip(low, -SHRINK, SHRINK), 2.0 * jnp.clip(high, -SHRINK, SHRINK)
            result.append(jnp.where(s > 0, low, 0.0) - jnp.where(s < NS - 1, high, 0.0))
        return result

    mask_t[...] = jnp.zeros_like(mask_t)
    kn[...] = jnp.zeros_like(kn)

    def arrived(part, group_offset):
        for dy in range(NY):
            message(part, group_offset * NY + dy).wait_recv()

    def unpack(part, group, store):
        rows = [got[part, group * NY + i].astype(F32) for i in range(NY)]
        at = pl.multiple_of(group * R, 8)
        for j in range(2):
            tiles = [
                jnp.concatenate([rows[i][20 * k + 10 * j : 20 * k + 10 * j + 10] for i in range(NY)], axis=0)
                for k in range(5)
            ]
            store(j, at, apart(tiles))
        return rows, at

    def store_k(j, at, pair):
        kn[2 * j, pl.ds(at, R), :] = pair[0]
        kn[2 * j + 1, pl.ds(at, R), :] = pair[1]

    def unpack_k(group):
        rows, at = unpack(0, group, store_k)
        marks = []
        for i in range(NY):
            part = rows[i][100:104]
            marks += [part, pltpu.roll(part, 128 - R, 1), pltpu.roll(part, 128 - 2 * R, 1)[0:2]]
        x_t[pl.ds(at, R), :] = jnp.concatenate(marks, axis=0)

    def first_group(part):
        own_copies[part].wait()
        for dy in range(1, NY):
            message(part, dy).wait_recv()

    first_group(0)
    unpack_k(z)

    def next_k(dz, carry):
        arrived(0, dz)
        unpack_k(lax.rem(z + NZ - dz, NZ))
        return carry

    lax.fori_loop(1, NZ, next_k, 0)
    mk_out[...] = x_t[0:LP, :].T[0:R, 0:N].astype(BF16)
    masks = to_coil(lambda peer: mk_out, mk_in, mk_ss, mk_rs)
    mk_in[c] = mk_out[...]
    for j in range(2):
        for ch in range(2):
            kt[ch * N : ch * N + N, j * LP : j * LP + LP] = kn[2 * j + ch].T[0:N, :]
    for copy in chunked:
        copy.wait()
    state = []
    for ch in range(2):
        total = jnp.zeros((R, LP), F32)
        for peer in range(NC):
            piece = own_in[peer]
            piece = jnp.concatenate([piece if ch == 0 else pltpu.roll(piece, 64, 1)] + [jnp.zeros((R, 256), F32)], axis=1)
            piece = piece if peer == 0 else pltpu.roll(piece, R * peer, 1)
            total = jnp.where(jnp.logical_and(lanes >= R * peer, lanes < R * peer + R), piece, total)
        state.append(total)
        zex_out[0, ch * R : ch * R + R, :] = total
    neighbours = to_neighbours(0)
    for copy in gathered:
        copy.wait()
    for peer in range(NC):
        real, imag = apart_rows(ag_in[0, peer])
        kn[0, peer * R : peer * R + R, :] = real
        kn[1, peer * R : peer * R + R, :] = imag
    for ch in range(2):
        v[ch] = kn[ch].T[0:N, :]

    for copy in masks:
        copy.wait()
    for peer in range(NC):
        mask_t[peer * R : peer * R + R, 0:N] = mk_in[peer].astype(F32)
    for ch in range(2):
        for j in range(2):
            kt[ch * N : ch * N + N, j * LP : j * LP + LP] *= mask_t[...]
    for load in loads[2:]:
        load.wait()
    high, low = split_f32(kt[...])
    kt[...] = mm(li[...], high) + mm(li[...], low) + mm(lil[...], high)
    for j in range(2):
        columns = jnp.concatenate(
            [kt[0:N, j * LP : j * LP + LP], kt[N : 2 * N, j * LP : j * LP + LP]], axis=1)
        high, low = split_f32(columns)
        gadj[j] = mm(high, rinv[...]) + mm(low, rinv[...]) + mm(high, ril[...])

    def store_maps(j, at, pair):
        sens[j, 0, pl.ds(at, R), :] = pair[0]
        sens[j, 1, pl.ds(at, R), :] = pair[1]

    first_group(1)
    unpack(1, z, store_maps)

    def next_maps(dz, carry):
        arrived(1, dz)
        unpack(1, lax.rem(z + NZ - dz, NZ), store_maps)
        return carry

    lax.fori_loop(1, NZ, next_maps, 0)

    def conjugate_sum(rows, images):
        real, imag = None, None
        for j in range(2):
            a, b = images[j][:, 0:LP], images[j][:, LP : 2 * LP]
            re = sens[j, 0, rows] * a + sens[j, 1, rows] * b
            im = sens[j, 0, rows] * b - sens[j, 1, rows] * a
            real, imag = (re, im) if real is None else (real + re, imag + im)
        return real, imag

    adj[0], adj[1] = conjugate_sum(pl.ds(0, N), [gadj[0], gadj[1]])

    def forward_rows(at, vr, vi):
        rows = pl.ds(at, R)
        for j in range(2):
            mr, mi = sens[j, 0, rows], sens[j, 1, rows]
            both = mm(jnp.concatenate([mr * vr - mi * vi, mr * vi + mi * vr], axis=1).astype(BF16), rf[...])
            for ch in range(2):
                part = both[:, ch * LP : ch * LP + LP]
                stage_f[pl.ds(ch * N + at, R), j * LP : j * LP + LP] = part

    def reduce_to(step, peer):
        rows = pl.ds(pl.multiple_of(peer * R, 8), R)
        images = []
        for j in range(2):
            columns = jnp.concatenate(
                [stage_f[rows, j * LP : j * LP + LP],
                 stage_f[pl.ds(pl.multiple_of(N + peer * R, 8), R), j * LP : j * LP + LP]], axis=1)
            images.append(mm(columns.astype(BF16), rinv[...]))
        real, imag = conjugate_sum(rows, images)
        rs_out[step, peer] = beside((real - adj[0, rows])[:, 0:N], (imag - adj[1, rows])[:, 0:N]).astype(BF16)

    for step in range(2):
        if step == 0:
            for peer in range(NC):
                forward_rows(peer * R, v[0, peer * R : peer * R + R, :], v[1, peer * R : peer * R + R, :])
        else:
            forward_rows(pl.multiple_of(c * R, 8), *apart_rows(ag_out[1]))
            for i, copy in enumerate(regathered):
                copy.wait_recv()
                sender = lax.rem(c + NC - 1 - i, NC)
                forward_rows(pl.multiple_of(sender * R, 8), *apart_rows(ag_in[1, sender]))
        spectrum = mm(lf[...], stage_f[...].astype(BF16))
        for ch in range(2):
            for j in range(2):
                stage_b[ch * N : ch * N + N, j * LP : j * LP + LP] = (
                    spectrum[ch * N : ch * N + N, j * LP : j * LP + LP] * mask_t[...]).astype(BF16)
        stage_f[...] = mm(li[...], stage_b[...])
        reduced = []
        for i, peer in enumerate(coil_peers):
            reduce_to(step, peer)
            copy = pltpu.make_async_remote_copy(
                src_ref=rs_out.at[step, peer], dst_ref=rs_in.at[step, c], send_sem=rs_ss.at[step, i],
                recv_sem=rs_rs.at[step, i], device_id=(s, peer), device_id_type=MESH)
            copy.start()
            reduced.append(copy)
        reduce_to(step, c)
        for copy in neighbours:
            copy.wait()
        smooth = regular(state, zex_in.at[step], step == 1)
        data = rs_out[step, c].astype(F32)
        for i, copy in enumerate(reduced):
            copy.wait()
            data = data + rs_in[step, lax.rem(c + NC - 1 - i, NC)].astype(F32)
        data = apart([data[:, k * 128 : k * 128 + 128] for k in range(5)])
        state = [state[ch] - STEP_SIZE * (data[ch] + PENALTY * smooth[ch]) for ch in range(2)]
        if step == 0:
            ag_out[1] = beside(state[0][:, 0:N], state[1][:, 0:N]).astype(BF16)
            regathered = to_coil(lambda peer: ag_out.at[1], ag_in.at[1], ag_ss.at[1], ag_rs.at[1])
            zex_out[1] = jnp.concatenate(state, axis=0)
            neighbours = to_neighbours(1)

    coil_to = s // NY
    slot = lax.rem(s, NY)
    result = beside(state[0][:, 0:N], state[1][:, 0:N])

    def final_copy(t, at):
        return pltpu.make_async_remote_copy(
            src_ref=fin_out.at[t], dst_ref=fin_in.at[at], send_sem=fin_ss.at[t],
            recv_sem=fin_rs.at[at], device_id=(4 * c + t, coil_to), device_id_type=MESH)

    for t in range(4):
        is_self = jnp.logical_and(4 * c + t == s, coil_to == c)
        for k in range(5):
            fin_out[t, 10 * k : 10 * k + 10, :] = result[10 * t : 10 * t + 10, k * 128 : k * 128 + 128]

        @pl.when(jnp.logical_not(is_self))
        def _():
            final_copy(t, slot).start()

        @pl.when(is_self)
        def _():
            copy = pltpu.make_async_copy(fin_out.at[t], fin_in.at[slot], local_sem.at[2])
            copy.start()
            copy.wait()

    for copy in regathered:
        copy.wait_send()
    for part in range(2):

        def sent(i, carry):
            message(part, i + 1).wait_send()
            return carry

        lax.fori_loop(0, NS - 1, sent, 0)

    for t in range(4):
        is_self = jnp.logical_and(4 * c + t == s, coil_to == c)

        @pl.when(jnp.logical_not(is_self))
        def _():
            final_copy(t, t).wait()

        rows = fin_in[t]
        tiles = [rows[10 * k : 10 * k + 10] for k in range(5)]
        tiles[4] = tiles[4][:, 0:64], tiles[4][:, 64:128]
        for ch in range(2):
            out[ch, :, t, :] = jnp.concatenate([tiles[2 * ch], tiles[2 * ch + 1], tiles[4][ch]], axis=1)


def hand_over(prior_in, out_in, prior, out):
    prior[...] = prior_in[...]
    out[...] = out_in[...]


def local(
    noisy_image, noise_draw, block_routes, conv_in, bias_in, norm_gain, conv_mid, bias_mid, conv_out,
    coil_maps, kspace_data, sample_mask,
):
    tables = [jnp.asarray(table) for table in dft_tables()]
    vmem = pl.BlockSpec(memory_space=pltpu.VMEM)
    hbm = pl.BlockSpec(memory_space=pl.ANY)
    prior, out = pl.pallas_call(
        kernel,
        out_shape=(
            jax.ShapeDtypeStruct((2, 1, R, N), F32),
            jax.ShapeDtypeStruct((2, 10, 4, N), F32),
        ),
        in_specs=[vmem] * 10 + [hbm] * 8,
        out_specs=(vmem, vmem),
        scratch_shapes=[
            pltpu.VMEM((2, 2, 10, NS, N), F32),
            pltpu.VMEM((2, 2, 10, NS, N), F32),
            pltpu.VMEM((2 * N, 2 * N), BF16),
            pltpu.VMEM((2 * N, 2 * N), BF16),
            pltpu.VMEM((2 * N, 2 * N), BF16),
            pltpu.VMEM((2 * LP, 2 * LP), BF16),
            pltpu.VMEM((2 * LP, 2 * LP), BF16),
            pltpu.VMEM((2 * LP, 2 * LP), BF16),
            pltpu.VMEM((384, 128), F32),
            pltpu.VMEM((1536, 256), BF16),
            pltpu.VMEM((128, 384), F32),
            pltpu.VMEM((3, 128, 128), F32),
            pltpu.VMEM((NS * ROWS, 128), F32),
            pltpu.VMEM((2, NS, ROWS, 128), BF16),
            pltpu.VMEM((2, NS, ROWS, 128), BF16),
            pltpu.VMEM((2, 16, N), F32),
            pltpu.VMEM((2, 16, N), F32),
            pltpu.VMEM((128, LP), F32),
            pltpu.VMEM((LP + 16, 128), F32),
            pltpu.VMEM((N, 384), BF16),
            pltpu.VMEM((N, 44 * LP), BF16),
            pltpu.VMEM((44, N, 128), BF16),
            pltpu.VMEM((N, 384), F32),
            pltpu.VMEM((2, R, 2 * N), BF16),
            pltpu.VMEM((2, NC, R, 2 * N), BF16),
            pltpu.VMEM((NC, R, 128), F32),
            pltpu.VMEM((NC, R, 128), F32),
            pltpu.VMEM((2, N, LP), F32),
            pltpu.VMEM((2, 2 * R, LP), F32),
            pltpu.VMEM((2, 2, 2 * R, LP), F32),
            pltpu.VMEM((4, LP, LP), F32),
            pltpu.VMEM((R, N), BF16),
            pltpu.VMEM((NC, R, N), BF16),
            pltpu.VMEM((N, LP), F32),
            pltpu.VMEM((2 * N, 2 * LP), F32),
            pltpu.VMEM((2, N, 2 * LP), F32),
            pltpu.VMEM((2, 2, N, LP), F32),
            pltpu.VMEM((2, N, LP), F32),
            pltpu.VMEM((2 * N, 2 * LP), F32),
            pltpu.VMEM((2 * N, 2 * LP), BF16),
            pltpu.VMEM((2, NC, R, 2 * N), BF16),
            pltpu.VMEM((2, NC, R, 2 * N), BF16),
            pltpu.VMEM((4, 56, 128), F32),
            pltpu.VMEM((4, 56, 128), F32),
            pltpu.SemaphoreType.DMA((8,)),
            pltpu.SemaphoreType.DMA((2,)),
            pltpu.SemaphoreType.DMA((2,)),
            pltpu.SemaphoreType.DMA((2, NS - 1)),
            pltpu.SemaphoreType.DMA((2, NS - 1)),
            pltpu.SemaphoreType.DMA((NC - 1,)),
            pltpu.SemaphoreType.DMA((NC - 1,)),
            pltpu.SemaphoreType.DMA((2, 2)),
            pltpu.SemaphoreType.DMA((2, 2)),
            pltpu.SemaphoreType.DMA((NC - 1,)),
            pltpu.SemaphoreType.DMA((NC - 1,)),
            pltpu.SemaphoreType.DMA((2, NC - 1)),
            pltpu.SemaphoreType.DMA((2, NC - 1)),
            pltpu.SemaphoreType.DMA((2, NC - 1)),
            pltpu.SemaphoreType.DMA((2, NC - 1)),
            pltpu.SemaphoreType.DMA((4,)),
            pltpu.SemaphoreType.DMA((4,)),
            pltpu.SemaphoreType.DMA((3,)),
        ],
        compiler_params=pltpu.CompilerParams(
            collective_id=0, has_side_effects=True, vmem_limit_bytes=58 * 2**20
        ),
    )(
        noisy_image, noise_draw, block_routes, conv_in.transpose(0, 2, 1), bias_in.reshape(1, 128),
        norm_gain.reshape(1, 128), conv_mid, bias_mid.reshape(1, 128), conv_out, sample_mask,
        coil_maps.transpose(0, 1, 3, 2, 4), kspace_data.transpose(0, 1, 3, 2, 4), *tables,
    )
    prior, out = pl.pallas_call(
        hand_over,
        out_shape=(jax.ShapeDtypeStruct(prior.shape, F32), jax.ShapeDtypeStruct(out.shape, F32)),
        in_specs=[vmem, vmem],
        out_specs=(vmem, vmem),
    )(prior, out)
    refined = out.transpose(0, 2, 3, 1)
    return prior, refined


def solution(mesh):
    return jax.shard_map(
        local,
        mesh=mesh,
        in_specs=(
            P(None, "slab", "coil", None),
            P(None, "slab", "coil", None),
            P("slab", None),
            P(), P(), P(), P(), P(), P(),
            P(None, "coil", None, "slab", None),
            P(None, "coil", None, "slab", None),
            P("slab", None),
        ),
        out_specs=(P(None, "slab", "coil", None), P(None, "coil", None, "slab")),
        check_vma=False,
    )
```
